256 devices in a mesh: freq: 2 (over core), ma: 128 (over z, x, y).
Axes of the slice: x: 4, y: 4, z: 8, core: 2. Of those that a mesh axis runs over, the one named last changes fastest.
Arguments:
- visibility: float32 [4, 2048, 16384], P('freq', 'ma'), parts along dimension 0, may hold values from -6 to 6
- slot_mode: int32 [128], replicated, may hold values from 0 to 127, as said below
- mode_rank: int32 [128], replicated, may hold values from 8 to 64
- beam_svd: bfloat16 [256, 64, 65536], P(('freq', 'ma')), parts along dimension 0, may hold values from -0.0234375 to 0.0234375
- signal_eigen: float32 [256, 64], P(('freq', 'ma')), parts along dimension 0, may hold values from 0.1 to 10
- sky_map: bfloat16 [256, 64, 2402], P(('freq', 'ma')), parts along dimension 0, may hold values from -0.75 to 0.75
Outputs:
- alm: float32 [256, 2402], P(('freq', 'ma')), parts along dimension 0
The draws below stay inside these ranges and needn't reach their ends.
There are 2 independent parts, one for each index of `freq`. The reference program is written for one: setup_inputs(seed, part) draws one part's arguments, and reference() takes and returns one part's arrays. A program takes and returns all parts, laid end to end along the dimension named above; an argument that names none is the same for every part. Nothing has to cross between parts.
Inputs may be any that keep to these rules, and one draw needn't show every extreme that they name: `slot_mode`: a permutation of 0 to 127.
All inputs are finite; a program needn't handle non-finite values.
Results may differ from the reference program's by a relative error of at most 0.006.
Values may be sent and summed in bfloat16 or wider, within the bound.
A program may use at most 128 MiB of HBM per device.

```python
import math
import jax
import jax.numpy as jnp
from jax import lax

B = 16384
NT = 2048
RMAX = 64
M_DEV = 1
LALM = 2402
MPAIRS = 128
N_MA = 128


def draw_slot_mode(key, part):
    key = jax.random.fold_in(key, 11)
    order = jax.random.permutation(key, N_MA).astype(jnp.int32)
    slots = jnp.arange(MPAIRS, dtype=jnp.int32)
    device = slots // M_DEV
    within = slots % M_DEV
    placed = order[device]
    column = jnp.where(within % 2 == 0, placed, N_MA - 1 - placed)
    return (within * N_MA + column).astype(jnp.int32)


def draw_mode_rank(key, part):
    key = jax.random.fold_in(key, 12)
    index = jnp.arange(MPAIRS, dtype=jnp.int32)
    base = RMAX - 3 * RMAX // 4 * index // MPAIRS
    noise = jax.random.randint(key, (MPAIRS,), 0, max(RMAX // 8, 1), dtype=jnp.int32)
    ranks = jnp.maximum(base - noise, RMAX // 8)
    ranks = jnp.where(index == 0, RMAX, ranks)
    ranks = jnp.where(index == MPAIRS - 1, RMAX // 8, ranks)
    return ranks.astype(jnp.int32)


def steps_of(stream_key, dims, pieces, low, high):
    gain = 1.0
    for axis_at, blocks in pieces:
        steps = jax.random.uniform(jax.random.fold_in(jax.random.fold_in(stream_key, 6), axis_at), (blocks,), jnp.float32, low / len(pieces), high / len(pieces))
        gain = gain * jnp.repeat(jnp.exp(steps), dims[axis_at] // blocks).reshape((-1,) + (1,) * (len(dims) - 1 - axis_at))
    return gain


def centred(key, extent, spread, most, shards=(), kind=jnp.bfloat16):
    factor_of = steps_of(key, extent, shards, -0.22, 0.18) if shards else 1.0
    array = jax.random.normal(key, extent, jnp.float32) * spread * factor_of
    return jnp.minimum(jnp.maximum(array, -most), most).astype(kind)


def setup_inputs(seed: int = 0, part: int = 0) -> dict:
    key_of = jax.random.split(jax.random.key(seed), 7)
    own_keys = jax.random.split(jax.random.fold_in(key_of[6], part), 7)
    return {
        "visibility": centred(own_keys[0], (2, NT, B), 1.0, 6.0, ((1, 128),), jnp.float32),
        "slot_mode": draw_slot_mode(jax.random.fold_in(key_of[6], 71), part),
        "mode_rank": draw_mode_rank(jax.random.fold_in(key_of[6], 71), part),
        "beam_svd": centred(own_keys[3], (MPAIRS, RMAX, 4 * B), (4 * B) ** -0.5, 0.0234375, ((0, 128),)),
        "signal_eigen": jnp.clip(jnp.exp(math.log(10.0) - 4.6051702 * jax.random.uniform(own_keys[4], (MPAIRS, RMAX), jnp.float32) ** steps_of(own_keys[4], (MPAIRS, RMAX), ((0, 128),), -0.2, 0.2)), 0.1, 10.0),
        "sky_map": centred(own_keys[5], (MPAIRS, RMAX, LALM), RMAX ** -0.5, 0.75, ((0, 128),)),
    }


def trig_tables(slot_mode):
    steps = jnp.arange(NT, dtype=jnp.int32)
    wave = (slot_mode.astype(jnp.int32) + 1)[:, None]
    phase = (wave * steps[None, :] % NT).astype(jnp.float32) * jnp.float32(2.0 * math.pi / NT)
    return (jnp.cos(phase), jnp.sin(phase))

def reference(visibility, slot_mode, mode_rank, beam_svd, signal_eigen, sky_map):
    cos_table, sin_table = trig_tables(slot_mode)
    cos_sum = jnp.einsum('mt,ctb->mcb', cos_table, visibility, precision=lax.Precision.HIGHEST)
    sin_sum = jnp.einsum('mt,ctb->mcb', sin_table, visibility, precision=lax.Precision.HIGHEST)
    scale = jnp.float32(1.0 / math.sqrt(NT))
    modes = jnp.stack([cos_sum[:, 0] + sin_sum[:, 1], cos_sum[:, 1] - sin_sum[:, 0], cos_sum[:, 0] - sin_sum[:, 1], cos_sum[:, 1] + sin_sum[:, 0]], axis=1) * scale
    modes = modes.astype(jnp.bfloat16).reshape(MPAIRS, 4 * B)
    ranks = mode_rank[slot_mode]
    levels = jnp.arange(RMAX, dtype=jnp.int32)

    def one_slot(items):
        row, beam, eigen, mapping, rank = items
        projected = jnp.dot(beam, row, preferred_element_type=jnp.float32)
        weight = eigen / (1.0 + eigen)
        filtered = jnp.where(levels < rank, projected * weight, jnp.float32(0.0)).astype(jnp.bfloat16)
        return jnp.dot(filtered, mapping, preferred_element_type=jnp.float32)
    return lax.map(one_slot, (modes, beam_svd, signal_eigen, sky_map, ranks))
```

```python
import functools
import math

import jax
import jax.numpy as jnp
from jax import lax
from jax.experimental import pallas as pl
from jax.experimental.pallas import tpu as pltpu
from jax.sharding import PartitionSpec as P

MESH = pl.DeviceIdType.MESH
NZ, NX, NY = 8, 4, 4
NP = NX * NY
NSUB = 8
GSUB = 4
NG = NSUB // GSUB
W = 128
F32, BF16 = jnp.float32, jnp.bfloat16


def sin_cos(index, period):
    quarter = period // 4
    shifted = index + quarter // 2
    quadrant = (shifted // quarter) % 4
    small = (shifted % quarter) - quarter // 2
    a = small.astype(F32) * F32(2.0 * math.pi / period)
    a2 = a * a
    s = a * (1.0 + a2 * (-1.0 / 6 + a2 * (1.0 / 120 + a2 * (-1.0 / 5040 + a2 * (1.0 / 362880)))))
    c = 1.0 + a2 * (-0.5 + a2 * (1.0 / 24 + a2 * (-1.0 / 720 + a2 * (1.0 / 40320))))
    odd = (quadrant % 2) == 1
    sin = jnp.where(odd, c, s)
    cos = jnp.where(odd, s, c)
    sin = jnp.where(quadrant >= 2, -sin, sin)
    cos = jnp.where((quadrant == 1) | (quadrant == 2), -cos, cos)
    return sin, cos


def column_of(row, n):
    r = lax.broadcasted_iota(jnp.int32, (n, n), 0)
    c = lax.broadcasted_iota(jnp.int32, (n, n), 1)
    return jnp.sum(jnp.where(r == c, jnp.broadcast_to(row, (n, n)), 0.0), axis=1, keepdims=True)


def kernel(
    vis, slot, rank, beam, eigen, sky, out,
    vis_v, slot_v, rank_v, beam_v, eigen_v, sky_v,
    vb, xs, tab, part, zbuf, bbuf, fsum, ob, modes,
    vis_sem, small_sem, beam_sem, sky_sem,
    s1_send, s1_recv, z_send, za_recv, zf_recv, s3_send, s3_recv,
):
    i = lax.axis_index("ma")
    z, p = i // NP, i % NP
    x, y = p // NY, p % NY
    modes_total = slot.shape[1]
    times = vis.shape[1]
    total = times * NZ * NP
    plane_times = times * NP

    def plane(dx, dy):
        return ((x + dx) % NX) * NY + (y + dy) % NY

    def zdev(d):
        return {"ma": ((z + d + NZ) % NZ) * NP + p}

    offsets = [(dx, dy) for dx in (2, 1, 3, 0) for dy in (2, 1, 3, 0) if (dx, dy) != (0, 0)]
    zoffs = (1, -1, 2, -2)

    pieces = vis_sem.shape[0]
    span = vis.shape[2] // pieces
    for q in range(pieces):
        cols = pl.ds(q * span, span)
        pltpu.make_async_copy(vis.at[:, :, cols], vis_v.at[:, :, cols], vis_sem.at[q]).start()
    small = [(slot, slot_v), (rank, rank_v), (eigen, eigen_v)]
    for n, (src, dst) in enumerate(small):
        pltpu.make_async_copy(src, dst, small_sem.at[n]).start()

    barrier = pltpu.get_barrier_semaphore()
    for dx, dy in offsets:
        pl.semaphore_signal(barrier, 1, device_id={"ma": z * NP + plane(dx, dy)}, device_id_type=MESH)
    for d in zoffs:
        pl.semaphore_signal(barrier, 1, device_id=zdev(d), device_id_type=MESH)

    for q in range(pieces):
        cols = pl.ds(q * span, span)
        pltpu.make_async_copy(vis.at[:, :, cols], vis_v.at[:, :, cols], vis_sem.at[q]).wait()

        def cast(b, carry):
            for s in range(NSUB):
                for c in range(2):
                    at = pl.multiple_of(b * (NSUB * W) + s * W, W)
                    vb[s, b, :, c * W:(c + 1) * W] = vis_v[c, :, pl.ds(at, W)].astype(BF16)
            return carry

        per = NP // pieces
        lax.fori_loop(q * per, (q + 1) * per, cast, 0)
    pltpu.make_async_copy(beam.at[0], beam_v, beam_sem).start()
    pltpu.make_async_copy(sky.at[0], sky_v, sky_sem).start()

    pl.semaphore_wait(barrier, len(offsets) + len(zoffs))
    for s in range(NSUB):
        for dx, dy in offsets:
            to = plane(dx, dy)
            pltpu.make_async_remote_copy(
                src_ref=vb.at[s, to], dst_ref=xs.at[s, p], send_sem=s1_send.at[s], recv_sem=s1_recv.at[s],
                device_id={"ma": z * NP + to}, device_id_type=MESH,
            ).start()

    for s in range(NSUB):
        xs[s, p] = vb[s, p]
    for n, (src, dst) in enumerate(small):
        pltpu.make_async_copy(src, dst, small_sem.at[n]).wait()
    slot_f = slot_v[...].astype(F32)
    wave = (column_of(slot_f, modes_total) + 1.0).astype(jnp.int32)
    t = z * plane_times + lax.broadcasted_iota(jnp.int32, (modes_total, plane_times), 1)
    sin, cos = sin_cos((wave * t) % total, total)
    scale = F32(1.0 / math.sqrt(total))
    for n, table in enumerate((cos * scale, sin * scale)):
        high = table.astype(BF16)
        rows = pl.ds(n * modes_total, modes_total)
        tab[0, rows, :] = high
        tab[1, rows, :] = (table - high.astype(F32)).astype(BF16)
    lanes = lax.broadcasted_iota(jnp.int32, (1, modes_total), 1)
    own_mode = jnp.sum(jnp.where(lanes == i, slot_f, 0.0), axis=1, keepdims=True)
    own_rank = jnp.sum(
        jnp.where(lanes.astype(F32) == own_mode, rank_v[...].astype(F32), 0.0), axis=1, keepdims=True
    )
    levels = eigen_v.shape[1]
    eig = column_of(eigen_v[...], levels)
    level = lax.broadcasted_iota(jnp.int32, (levels, 1), 0).astype(F32)
    weight = jnp.where(level < own_rank, eig / (1.0 + eig), 0.0)

    def z_copy(src, dst, d, s, recv):
        return pltpu.make_async_remote_copy(
            src_ref=src, dst_ref=dst, send_sem=z_send.at[s], recv_sem=recv.at[s],
            device_id=zdev(d), device_id_type=MESH,
        )

    def zrow(d):
        return (z + d + NZ) % NZ

    def stage_a(s):
        blocks = pl.ds(0, NP - 1)
        pltpu.make_async_copy(xs.at[s, blocks], xs.at[s, blocks], s1_recv.at[s]).wait()
        block = xs[s].reshape(plane_times, 2 * W)
        res = jnp.dot(tab[0], block, preferred_element_type=F32) + jnp.dot(
            tab[1], block, preferred_element_type=F32
        )
        m = modes_total
        cr, ci, sr, si = res[:m, :W], res[:m, W:], res[m:, :W], res[m:, W:]
        for n, v in enumerate((cr + si, ci - sr, cr - si, ci + sr)):
            part[s, :, n] = v.astype(BF16).reshape(NZ, NP, W)
        far = 2 if s % 2 == 0 else -2
        z_copy(part.at[s, zrow(4)], zbuf.at[s, 2], far, s, za_recv).start()
        z_copy(part.at[s, zrow(3)], zbuf.at[s, 0], 1, s, za_recv).start()
        z_copy(part.at[s, zrow(-3)], zbuf.at[s, 1], -1, s, za_recv).start()
        z_copy(part.at[s, zrow(1)], zbuf.at[s, 3], 1, s, zf_recv).start()
        z_copy(part.at[s, zrow(-1)], zbuf.at[s, 4], -1, s, zf_recv).start()

    def stage_b(s):
        three = pl.ds(0, 3)
        pltpu.make_async_copy(zbuf.at[s, three], zbuf.at[s, three], za_recv.at[s]).wait()
        for n, d in enumerate((2, -2)):
            v = part[s, zrow(d)].astype(F32) + zbuf[s, n].astype(F32)
            if (s % 2 == 0) == (n == 0):
                v = v + zbuf[s, 2].astype(F32)
            bbuf[s, n] = v.astype(BF16)
            z_copy(bbuf.at[s, n], zbuf.at[s, 5 + n], d, s, zf_recv).start()

    def stage_f(s):
        four = pl.ds(3, 4)
        pltpu.make_async_copy(zbuf.at[s, four], zbuf.at[s, four], zf_recv.at[s]).wait()
        v = part[s, z].astype(F32)
        for n in range(3, 7):
            v = v + zbuf[s, n].astype(F32)
        for n in range(4):
            fsum[:, (s % GSUB) * 4 + n, :] = v[n]
        if s % GSUB == GSUB - 1:
            g = s // GSUB
            ob[g] = fsum[...].astype(BF16)
            for dx, dy in offsets:
                to = plane(dx, dy)
                pltpu.make_async_remote_copy(
                    src_ref=ob.at[g, to], dst_ref=modes.at[g, p], send_sem=s3_send.at[g],
                    recv_sem=s3_recv.at[g], device_id={"ma": z * NP + to}, device_id_type=MESH,
                ).start()
            modes[g, p] = ob[g, p]

    baselines = vis.shape[2]

    def project(g, acc):
        blocks = pl.ds(0, NP - 1)
        pltpu.make_async_copy(modes.at[g, blocks], modes.at[g, blocks], s3_recv.at[g]).wait()

        def one(b, acc):
            rows = modes[g, b].astype(F32)
            for s in range(GSUB):
                for n in range(4):
                    at = pl.multiple_of(n * baselines + b * (NSUB * W) + (g * GSUB + s) * W, W)
                    r = s * 4 + n
                    acc = acc + beam_v[:, pl.ds(at, W)].astype(F32) * rows[r:r + 1, :]
            return acc

        return lax.fori_loop(0, NP, one, acc)

    for step in range(NSUB + 6):
        if step < NSUB:
            stage_a(step)
        if 0 <= step - 3 < NSUB:
            stage_b(step - 3)
        if 0 <= step - 6 < NSUB:
            stage_f(step - 6)
        if step == NSUB + 3:
            pltpu.make_async_copy(beam.at[0], beam_v, beam_sem).wait()
            pltpu.make_async_copy(sky.at[0], sky_v, sky_sem).wait()
            acc = project(0, jnp.zeros((levels, W), F32))
    for g in range(1, NG):
        acc = project(g, acc)
    filtered = jnp.sum(acc, axis=1, keepdims=True) * weight
    out[...] = jnp.sum(sky_v[...].astype(F32) * filtered, axis=0, keepdims=True)

    for s in range(NSUB):
        blocks = pl.ds(0, NP - 1)
        pltpu.make_async_copy(vb.at[s, blocks], vb.at[s, blocks], s1_send.at[s]).wait()
        pltpu.make_async_copy(zbuf.at[s], zbuf.at[s], z_send.at[s]).wait()
    for g in range(NG):
        blocks = pl.ds(0, NP - 1)
        pltpu.make_async_copy(ob.at[g, blocks], ob.at[g, blocks], s3_send.at[g]).wait()


def per_device(visibility, slot_mode, mode_rank, beam_svd, signal_eigen, sky_map):
    count = slot_mode.shape[0]
    levels, entries = beam_svd.shape[1:]
    multipoles = sky_map.shape[2]
    times = visibility.shape[1]
    any_spec = pl.BlockSpec(memory_space=pl.ANY)
    dma = pltpu.SemaphoreType.DMA
    return pl.pallas_call(
        kernel,
        out_shape=jax.ShapeDtypeStruct((1, multipoles), F32),
        in_specs=[any_spec] * 6,
        out_specs=pl.BlockSpec(memory_space=pltpu.VMEM),
        scratch_shapes=[
            pltpu.VMEM(visibility.shape, F32),
            pltpu.VMEM((1, count), jnp.int32),
            pltpu.VMEM((1, count), jnp.int32),
            pltpu.VMEM((levels, entries), BF16),
            pltpu.VMEM((1, levels), F32),
            pltpu.VMEM((levels, multipoles), BF16),
            pltpu.VMEM((NSUB, NP, times, 2 * W), BF16),
            pltpu.VMEM((NSUB, NP, times, 2 * W), BF16),
            pltpu.VMEM((2, 2 * count, times * NP), BF16),
            pltpu.VMEM((NSUB, NZ, 4, NP, W), BF16),
            pltpu.VMEM((NSUB, 7, 4, NP, W), BF16),
            pltpu.VMEM((NSUB, 2, 4, NP, W), BF16),
            pltpu.VMEM((NP, 4 * GSUB, W), F32),
            pltpu.VMEM((NG, NP, 4 * GSUB, W), BF16),
            pltpu.VMEM((NG, NP, 4 * GSUB, W), BF16),
            dma((4,)), dma((3,)), dma, dma,
            dma((NSUB,)), dma((NSUB,)), dma((NSUB,)), dma((NSUB,)), dma((NSUB,)), dma((NG,)), dma((NG,)),
        ],
        compiler_params=pltpu.CompilerParams(
            collective_id=0, has_side_effects=True, vmem_limit_bytes=60 * 2**20
        ),
    )(
        visibility, slot_mode.reshape(1, count), mode_rank.reshape(1, count), beam_svd, signal_eigen, sky_map
    )


def solution(mesh):
    return jax.shard_map(
        per_device,
        mesh=mesh,
        in_specs=(
            P("freq", "ma", None),
            P(),
            P(),
            P(("freq", "ma"), None, None),
            P(("freq", "ma"), None),
            P(("freq", "ma"), None, None),
        ),
        out_specs=P(("freq", "ma"), None),
        check_vma=False,
    )
```

```python
import functools
import math

import jax
import jax.numpy as jnp
from jax import lax
from jax.experimental import pallas as pl
from jax.experimental.pallas import tpu as pltpu
from jax.sharding import PartitionSpec as P

MESH = pl.DeviceIdType.MESH
NZ, NX, NY = 8, 4, 4
NP = NX * NY
NSUB = 8
GSUB = 4
NG = NSUB // GSUB
W = 128
F32, BF16 = jnp.float32, jnp.bfloat16

CHAIN = {4: 3, 3: 2, 2: 1, 1: 0}
THREE = {4: 3, 3: 1, 2: 1, 1: 0}
TREE = {4: 2, 3: 2, 2: 0, 1: 0}
DIRECT = {4: 0, 3: 0, 2: 0, 1: 0}
AHEAD = 4
PLANS = (TREE,) * 7 + (DIRECT,)
LEVELS = 5
NODES = ((1, 3), (-1, 3), (0, 4), (1, 2), (-1, 2), (1, 1), (-1, 1))


def z_plan(s):
    sign4 = 1 if s % 2 == 0 else -1
    parent = PLANS[s]
    nodes = [(side or sign4, d, slot) for slot, (side, d) in enumerate(NODES)]

    def children(sign, d):
        return [n for n in nodes if d and n[0] == sign and parent[n[1]] == d]

    def level(sign, d):
        below = [n for n in nodes if parent[n[1]] == 0] if d == 0 else children(sign, d)
        return max((1 + level(n[0], n[1]) for n in below), default=0)

    last = level(0, 0)
    sends = [[] for _ in range(last)]
    counts = [0] * (last + 1)
    for sign, d, slot in nodes:
        to = parent[d]
        to_level = level(sign if to else 0, to)
        counts[to_level] += 1
        sends[level(sign, d)].append((slot, sign, d, to, to_level, [n[2] for n in children(sign, d)]))
    for group in sends:
        group.sort(key=lambda n: -n[2])
    arrivals = [n[2] for n in nodes if parent[n[1]] == 0]
    return last, sends, counts, arrivals


def schedule():
    events = []
    for s in range(NSUB):
        last, sends, _, _ = z_plan(s)
        ready = [S_FIRST + S_EACH * s] + [0.0] * last
        for k in range(last + 1):
            events.append((ready[k], s, k))
            for _, _, d, to, to_level, _ in (sends[k] if k < last else ()):
                ready[to_level] = max(ready[to_level], ready[k] + HOP + LINK * (d - to))
    return [(s, k) for _, s, k in sorted(events)]


S_FIRST, S_EACH, HOP, LINK = 5.0, 1.43, 4.0, 0.8


def sin_cos(index, period):
    quarter = period // 4
    shifted = index + quarter // 2
    quadrant = (shifted // quarter) % 4
    small = (shifted % quarter) - quarter // 2
    a = small.astype(F32) * F32(2.0 * math.pi / period)
    a2 = a * a
    s = a * (1.0 + a2 * (-1.0 / 6 + a2 * (1.0 / 120 + a2 * (-1.0 / 5040 + a2 * (1.0 / 362880)))))
    c = 1.0 + a2 * (-0.5 + a2 * (1.0 / 24 + a2 * (-1.0 / 720 + a2 * (1.0 / 40320))))
    odd = (quadrant % 2) == 1
    sin = jnp.where(odd, c, s)
    cos = jnp.where(odd, s, c)
    sin = jnp.where(quadrant >= 2, -sin, sin)
    cos = jnp.where((quadrant == 1) | (quadrant == 2), -cos, cos)
    return sin, cos


def column_of(row, n):
    r = lax.broadcasted_iota(jnp.int32, (n, n), 0)
    c = lax.broadcasted_iota(jnp.int32, (n, n), 1)
    return jnp.sum(jnp.where(r == c, jnp.broadcast_to(row, (n, n)), 0.0), axis=1, keepdims=True)


def kernel(
    vis, slot, rank, beam, eigen, sky, out,
    vis_v, slot_v, rank_v, beam_v, eigen_v, sky_v,
    vb, xs, tab, part, zbuf, bbuf, fsum, ob, modes,
    vis_sem, small_sem, beam_sem, sky_sem,
    s1_send, s1_recv, z_send, z_recv, s3_send, s3_recv,
):
    i = lax.axis_index("ma")
    z, p = i // NP, i % NP
    x, y = p // NY, p % NY
    modes_total = slot.shape[1]
    times = vis.shape[1]
    total = times * NZ * NP
    plane_times = times * NP

    def plane(dx, dy):
        return ((x + dx) % NX) * NY + (y + dy) % NY

    def zdev(d):
        return {"ma": ((z + d + NZ) % NZ) * NP + p}

    offsets = sorted(
        ((dx, dy) for dx in range(NX) for dy in range(NY) if (dx, dy) != (0, 0)),
        key=lambda o: -min(o[0], NX - o[0]) - min(o[1], NY - o[1]),
    )
    hops = {sign * (d - to) for s in range(NSUB) for group in z_plan(s)[1] for _, sign, d, to, _, _ in group}
    zoffs = sorted({h % NZ for h in hops} | {-h % NZ for h in hops})

    pieces = vis_sem.shape[0]
    span = vis.shape[2] // pieces
    for q in range(pieces):
        cols = pl.ds(q * span, span)
        pltpu.make_async_copy(vis.at[:, :, cols], vis_v.at[:, :, cols], vis_sem.at[q]).start()
    small = [(slot, slot_v), (rank, rank_v), (eigen, eigen_v)]
    for n, (src, dst) in enumerate(small):
        pltpu.make_async_copy(src, dst, small_sem.at[n]).start()

    barrier = pltpu.get_barrier_semaphore()
    for dx, dy in offsets:
        pl.semaphore_signal(barrier, 1, device_id={"ma": z * NP + plane(dx, dy)}, device_id_type=MESH)
    for d in zoffs:
        pl.semaphore_signal(barrier, 1, device_id=zdev(d), device_id_type=MESH)

    for q in range(pieces):
        cols = pl.ds(q * span, span)
        pltpu.make_async_copy(vis.at[:, :, cols], vis_v.at[:, :, cols], vis_sem.at[q]).wait()

        def cast(b, carry):
            for s in range(NSUB):
                for c in range(2):
                    at = pl.multiple_of(b * (NSUB * W) + s * W, W)
                    vb[s, b, :, c * W:(c + 1) * W] = vis_v[c, :, pl.ds(at, W)].astype(BF16)
            return carry

        per = NP // pieces
        lax.fori_loop(q * per, (q + 1) * per, cast, 0)
    pltpu.make_async_copy(beam.at[0], beam_v, beam_sem).start()
    pltpu.make_async_copy(sky.at[0], sky_v, sky_sem).start()

    pl.semaphore_wait(barrier, len(offsets) + len(zoffs))
    def send_sub(s, carry):
        for dx, dy in offsets:
            to = plane(dx, dy)
            pltpu.make_async_remote_copy(
                src_ref=vb.at[s, to], dst_ref=xs.at[s, p], send_sem=s1_send.at[s], recv_sem=s1_recv.at[s],
                device_id={"ma": z * NP + to}, device_id_type=MESH,
            ).start()
        return carry

    lax.fori_loop(0, AHEAD, send_sub, 0)

    for s in range(NSUB):
        xs[s, p] = vb[s, p]
    for n, (src, dst) in enumerate(small):
        pltpu.make_async_copy(src, dst, small_sem.at[n]).wait()
    slot_f = slot_v[...].astype(F32)
    wave = (column_of(slot_f, modes_total) + 1.0).astype(jnp.int32)
    t = z * plane_times + lax.broadcasted_iota(jnp.int32, (modes_total, plane_times), 1)
    sin, cos = sin_cos((wave * t) % total, total)
    scale = F32(1.0 / math.sqrt(total))
    for n, table in enumerate((cos * scale, sin * scale)):
        high = table.astype(BF16)
        rows = pl.ds(n * modes_total, modes_total)
        tab[0, rows, :] = high
        tab[1, rows, :] = (table - high.astype(F32)).astype(BF16)
    lanes = lax.broadcasted_iota(jnp.int32, (1, modes_total), 1)
    own_mode = jnp.sum(jnp.where(lanes == i, slot_f, 0.0), axis=1, keepdims=True)
    own_rank = jnp.sum(
        jnp.where(lanes.astype(F32) == own_mode, rank_v[...].astype(F32), 0.0), axis=1, keepdims=True
    )
    levels = eigen_v.shape[1]
    eig = column_of(eigen_v[...], levels)
    level = lax.broadcasted_iota(jnp.int32, (levels, 1), 0).astype(F32)
    weight = jnp.where(level < own_rank, eig / (1.0 + eig), 0.0)

    def zrow(d):
        return (z + d + NZ) % NZ

    def transform(s):
        blocks = pl.ds(0, NP - 1)
        pltpu.make_async_copy(xs.at[s, blocks], xs.at[s, blocks], s1_recv.at[s]).wait()
        if s + AHEAD < NSUB:
            send_sub(s + AHEAD, 0)
        block = xs[s].reshape(plane_times, 2 * W)
        res = jnp.dot(tab[0], block, preferred_element_type=F32) + jnp.dot(
            tab[1], block, preferred_element_type=F32
        )
        m = modes_total
        cr, ci, sr, si = res[:m, :W], res[:m, W:], res[m:, :W], res[m:, W:]
        for n, v in enumerate((cr + si, ci - sr, cr - si, ci + sr)):
            part[s, :, n] = v.astype(BF16).reshape(NZ, NP, W)

    def z_step(s, k):
        last, sends, counts, arrivals = z_plan(s)
        if k == 0:
            transform(s)
        else:
            some = pl.ds(0, counts[k])
            pltpu.make_async_copy(zbuf.at[s, some], zbuf.at[s, some], z_recv.at[s, k]).wait()
        if k == last:
            v = part[s, z].astype(F32)
            for slot in arrivals:
                v = v + zbuf[s, slot].astype(F32)
            for n in range(4):
                fsum[s // GSUB, :, (s % GSUB) * 4 + n, :] = v[n]
            return
        for slot, sign, d, to, to_level, below in sends[k]:
            src = part.at[s, zrow(sign * d)]
            if below:
                v = src[...].astype(F32)
                for c in below:
                    v = v + zbuf[s, c].astype(F32)
                src = bbuf.at[s, slot]
                src[...] = v.astype(BF16)
            pltpu.make_async_remote_copy(
                src_ref=src, dst_ref=zbuf.at[s, slot], send_sem=z_send.at[s], recv_sem=z_recv.at[s, to_level],
                device_id=zdev(sign * (d - to)), device_id_type=MESH,
            ).start()

    def exchange(g):
        ob[g] = fsum[g].astype(BF16)
        for n, (dx, dy) in enumerate(offsets):
            to = plane(dx, dy)
            pltpu.make_async_remote_copy(
                src_ref=ob.at[g, to], dst_ref=modes.at[g, p], send_sem=s3_send.at[g],
                recv_sem=s3_recv.at[g, n], device_id={"ma": z * NP + to}, device_id_type=MESH,
            ).start()

    baselines = vis.shape[2]

    def project_one(b, rows, g, acc):
        for s in range(GSUB):
            for n in range(4):
                at = pl.multiple_of(n * baselines + b * (NSUB * W) + (g * GSUB + s) * W, W)
                r = s * 4 + n
                acc = acc + beam_v[:, pl.ds(at, W)].astype(F32) * rows[r:r + 1, :]
        return acc

    def project(g, acc):
        acc = project_one(p, ob[g, p].astype(F32), g, acc)
        for n in reversed(range(len(offsets))):
            dx, dy = offsets[n]
            b = plane(NX - dx, NY - dy)
            pltpu.make_async_copy(modes.at[g, b], modes.at[g, b], s3_recv.at[g, n]).wait()
            acc = project_one(b, modes[g, b].astype(F32), g, acc)
        return acc

    done = [0] * NG
    for s, k in schedule():
        z_step(s, k)
        if k == z_plan(s)[0]:
            g = s // GSUB
            done[g] += 1
            if done[g] == GSUB:
                exchange(g)
    pltpu.make_async_copy(beam.at[0], beam_v, beam_sem).wait()
    pltpu.make_async_copy(sky.at[0], sky_v, sky_sem).wait()
    acc = jnp.zeros((levels, W), F32)
    for g in range(NG):
        acc = project(g, acc)
    filtered = jnp.sum(acc, axis=1, keepdims=True) * weight
    out[...] = jnp.sum(sky_v[...].astype(F32) * filtered, axis=0, keepdims=True)

    for s in range(NSUB):
        blocks = pl.ds(0, NP - 1)
        pltpu.make_async_copy(vb.at[s, blocks], vb.at[s, blocks], s1_send.at[s]).wait()
        pltpu.make_async_copy(zbuf.at[s], zbuf.at[s], z_send.at[s]).wait()
    for g in range(NG):
        blocks = pl.ds(0, NP - 1)
        pltpu.make_async_copy(ob.at[g, blocks], ob.at[g, blocks], s3_send.at[g]).wait()


def per_device(visibility, slot_mode, mode_rank, beam_svd, signal_eigen, sky_map):
    count = slot_mode.shape[0]
    levels, entries = beam_svd.shape[1:]
    multipoles = sky_map.shape[2]
    times = visibility.shape[1]
    any_spec = pl.BlockSpec(memory_space=pl.ANY)
    dma = pltpu.SemaphoreType.DMA
    return pl.pallas_call(
        kernel,
        out_shape=jax.ShapeDtypeStruct((1, multipoles), F32),
        in_specs=[any_spec] * 6,
        out_specs=pl.BlockSpec(memory_space=pltpu.VMEM),
        scratch_shapes=[
            pltpu.VMEM(visibility.shape, F32),
            pltpu.VMEM((1, count), jnp.int32),
            pltpu.VMEM((1, count), jnp.int32),
            pltpu.VMEM((levels, entries), BF16),
            pltpu.VMEM((1, levels), F32),
            pltpu.VMEM((levels, multipoles), BF16),
            pltpu.VMEM((NSUB, NP, times, 2 * W), BF16),
            pltpu.VMEM((NSUB, NP, times, 2 * W), BF16),
            pltpu.VMEM((2, 2 * count, times * NP), BF16),
            pltpu.VMEM((NSUB, NZ, 4, NP, W), BF16),
            pltpu.VMEM((NSUB, 7, 4, NP, W), BF16),
            pltpu.VMEM((NSUB, 7, 4, NP, W), BF16),
            pltpu.VMEM((NG, NP, 4 * GSUB, W), F32),
            pltpu.VMEM((NG, NP, 4 * GSUB, W), BF16),
            pltpu.VMEM((NG, NP, 4 * GSUB, W), BF16),
            dma((4,)), dma((3,)), dma, dma,
            dma((NSUB,)), dma((NSUB,)), dma((NSUB,)), dma((NSUB, LEVELS)), dma((NG,)), dma((NG, NP - 1)),
        ],
        compiler_params=pltpu.CompilerParams(
            collective_id=0, has_side_effects=True, vmem_limit_bytes=60 * 2**20
        ),
    )(
        visibility, slot_mode.reshape(1, count), mode_rank.reshape(1, count), beam_svd, signal_eigen, sky_map
    )


def solution(mesh):
    return jax.shard_map(
        per_device,
        mesh=mesh,
        in_specs=(
            P("freq", "ma", None),
            P(),
            P(),
            P(("freq", "ma"), None, None),
            P(("freq", "ma"), None),
            P(("freq", "ma"), None, None),
        ),
        out_specs=P(("freq", "ma"), None),
        check_vma=False,
    )
```

```python
import functools
import math

import jax
import jax.numpy as jnp
from jax import lax
from jax.experimental import pallas as pl
from jax.experimental.pallas import tpu as pltpu
from jax.sharding import PartitionSpec as P

MESH = pl.DeviceIdType.MESH
NZ, NX, NY = 8, 4, 4
NP = NX * NY
NSUB = 8
GSUB = 4
NG = NSUB // GSUB
W = 128
F32, BF16 = jnp.float32, jnp.bfloat16

CHAIN = {4: 3, 3: 2, 2: 1, 1: 0}
THREE = {4: 3, 3: 1, 2: 1, 1: 0}
TREE = {4: 2, 3: 2, 2: 0, 1: 0}
DIRECT = {4: 0, 3: 0, 2: 0, 1: 0}
SINGLES = 4
PAIRS = (NSUB - SINGLES) // 2
PLANS = (TREE,) * SINGLES
LEVELS = 5
PAIR_HOPS = (4, 3, -3, 2, -2, 1, -1)
NODES = ((1, 3), (-1, 3), (0, 4), (1, 2), (-1, 2), (1, 1), (-1, 1))


def z_plan(s):
    sign4 = 1 if s % 2 == 0 else -1
    parent = PLANS[s]
    nodes = [(side or sign4, d, slot) for slot, (side, d) in enumerate(NODES)]

    def children(sign, d):
        return [n for n in nodes if d and n[0] == sign and parent[n[1]] == d]

    def level(sign, d):
        below = [n for n in nodes if parent[n[1]] == 0] if d == 0 else children(sign, d)
        return max((1 + level(n[0], n[1]) for n in below), default=0)

    last = level(0, 0)
    sends = [[] for _ in range(last)]
    counts = [0] * (last + 1)
    for sign, d, slot in nodes:
        to = parent[d]
        to_level = level(sign if to else 0, to)
        counts[to_level] += 1
        sends[level(sign, d)].append((slot, sign, d, to, to_level, [n[2] for n in children(sign, d)]))
    for group in sends:
        group.sort(key=lambda n: -n[2])
    arrivals = [n[2] for n in nodes if parent[n[1]] == 0]
    return last, sends, counts, arrivals


def schedule():
    events = []
    for s in range(SINGLES):
        for k in range(z_plan(s)[0] + 1):
            events.append((S_EACH * s + (FIRST + LATER * (k - 1) if k else 0.0), s, k))
    for g in range(PAIRS):
        t = S_EACH * (SINGLES + 1 + 2 * g)
        events += [(t, g, "start"), (t + PAIR_COPY, g, "end")]
    return [(s, k) for _, s, k in sorted(events, key=lambda e: e[0])]


S_EACH, FIRST, LATER, PAIR_COPY = 1.43, 4.2, 4.6, 8.0


def sin_cos(index, period):
    quarter = period // 4
    shifted = index + quarter // 2
    quadrant = (shifted // quarter) % 4
    small = (shifted % quarter) - quarter // 2
    a = small.astype(F32) * F32(2.0 * math.pi / period)
    a2 = a * a
    s = a * (1.0 + a2 * (-1.0 / 6 + a2 * (1.0 / 120 + a2 * (-1.0 / 5040 + a2 * (1.0 / 362880)))))
    c = 1.0 + a2 * (-0.5 + a2 * (1.0 / 24 + a2 * (-1.0 / 720 + a2 * (1.0 / 40320))))
    odd = (quadrant % 2) == 1
    sin = jnp.where(odd, c, s)
    cos = jnp.where(odd, s, c)
    sin = jnp.where(quadrant >= 2, -sin, sin)
    cos = jnp.where((quadrant == 1) | (quadrant == 2), -cos, cos)
    return sin, cos


def column_of(row, n):
    r = lax.broadcasted_iota(jnp.int32, (n, n), 0)
    c = lax.broadcasted_iota(jnp.int32, (n, n), 1)
    return jnp.sum(jnp.where(r == c, jnp.broadcast_to(row, (n, n)), 0.0), axis=1, keepdims=True)


def kernel(
    vis, slot, rank, beam, eigen, sky, out,
    vis_v, slot_v, rank_v, beam_v, eigen_v, sky_v,
    vb, xs, tab, part, zbuf, bbuf, fsum, ob, modes,
    vis_sem, small_sem, beam_sem, sky_sem,
    s1_send, s1_recv, z_send, z_recv, s3_send, s3_recv,
    pv, xp, zp, pair_send, pair_recv, s1p_send, s1p_recv, zp_send, zp_recv,
):
    i = lax.axis_index("ma")
    z, p = i // NP, i % NP
    x, y = p // NY, p % NY
    modes_total = slot.shape[1]
    times = vis.shape[1]
    total = times * NZ * NP
    plane_times = times * NP

    def plane(dx, dy):
        return ((x + dx) % NX) * NY + (y + dy) % NY

    def zdev(d):
        return {"ma": ((z + d + NZ) % NZ) * NP + p}

    offsets = sorted(
        ((dx, dy) for dx in range(NX) for dy in range(NY) if (dx, dy) != (0, 0)),
        key=lambda o: -min(o[0], NX - o[0]) - min(o[1], NY - o[1]),
    )
    hops = {sign * (d - to) for s in range(SINGLES) for group in z_plan(s)[1] for _, sign, d, to, _, _ in group}
    hops |= set(range(1, NZ)) if PAIRS else set()
    zoffs = sorted({h % NZ for h in hops} | {-h % NZ for h in hops})

    pieces = vis_sem.shape[0]
    span = vis.shape[2] // pieces
    for q in range(pieces):
        cols = pl.ds(q * span, span)
        pltpu.make_async_copy(vis.at[:, :, cols], vis_v.at[:, :, cols], vis_sem.at[q]).start()
    small = [(slot, slot_v), (rank, rank_v), (eigen, eigen_v)]
    for n, (src, dst) in enumerate(small):
        pltpu.make_async_copy(src, dst, small_sem.at[n]).start()

    def zrow(d):
        return (z + d + NZ) % NZ

    barrier = pltpu.get_barrier_semaphore()
    for dx, dy in offsets:
        pl.semaphore_signal(barrier, 1, device_id={"ma": z * NP + plane(dx, dy)}, device_id_type=MESH)
    for d in zoffs:
        pl.semaphore_signal(barrier, 1, device_id=zdev(d), device_id_type=MESH)

    for q in range(pieces):
        cols = pl.ds(q * span, span)
        pltpu.make_async_copy(vis.at[:, :, cols], vis_v.at[:, :, cols], vis_sem.at[q]).wait()

        def cast(b, carry):
            for s in range(NSUB):
                for c in range(2):
                    at = pl.multiple_of(b * (NSUB * W) + s * W, W)
                    vb[s, b, :, c * W:(c + 1) * W] = vis_v[c, :, pl.ds(at, W)].astype(BF16)
            return carry

        per = NP // pieces
        lax.fori_loop(q * per, (q + 1) * per, cast, 0)
    pltpu.make_async_copy(beam.at[0], beam_v, beam_sem).start()
    pltpu.make_async_copy(sky.at[0], sky_v, sky_sem).start()

    pl.semaphore_wait(barrier, len(offsets) + len(zoffs))
    upper = [(z + g) % 2 for g in range(PAIRS)]
    kept = [SINGLES + 2 * g + upper[g] for g in range(PAIRS)]
    given = [SINGLES + 2 * g + 1 - upper[g] for g in range(PAIRS)]
    other = [1 - 2 * upper[g] for g in range(PAIRS)]

    for g in range(PAIRS):
        pltpu.make_async_remote_copy(
            src_ref=vb.at[given[g]], dst_ref=pv.at[g], send_sem=pair_send.at[g], recv_sem=pair_recv.at[g],
            device_id=zdev(other[g]), device_id_type=MESH,
        ).start()

    def send_blocks(src, dst, send_sem, recv_sem):
        for dx, dy in offsets:
            to = plane(dx, dy)
            pltpu.make_async_remote_copy(
                src_ref=src.at[to], dst_ref=dst.at[p], send_sem=send_sem, recv_sem=recv_sem,
                device_id={"ma": z * NP + to}, device_id_type=MESH,
            ).start()

    def send_single(s, carry):
        send_blocks(vb.at[s], xs.at[s], s1_send.at[s], s1_recv.at[s])
        return carry

    lax.fori_loop(0, SINGLES, send_single, 0)
    for g in range(PAIRS):
        send_blocks(vb.at[kept[g]], xp.at[g, 0], s1p_send.at[g], s1p_recv.at[g])

    for s in range(SINGLES):
        xs[s, p] = vb[s, p]
    for g in range(PAIRS):
        xp[g, 0, p] = vb[kept[g], p]
    for n, (src, dst) in enumerate(small):
        pltpu.make_async_copy(src, dst, small_sem.at[n]).wait()
    slot_f = slot_v[...].astype(F32)
    wave = (column_of(slot_f, modes_total) + 1.0).astype(jnp.int32)
    scale = F32(1.0 / math.sqrt(total))
    for q, d in enumerate([0] + other):
        t = zrow(d) * plane_times + lax.broadcasted_iota(jnp.int32, (modes_total, plane_times), 1)
        sin, cos = sin_cos((wave * t) % total, total)
        for n, table in enumerate((cos * scale, sin * scale)):
            high = table.astype(BF16)
            rows = pl.ds(n * modes_total, modes_total)
            tab[q, 0, rows, :] = high
            tab[q, 1, rows, :] = (table - high.astype(F32)).astype(BF16)
    for g in range(PAIRS):
        pltpu.make_async_copy(pv.at[g], pv.at[g], pair_recv.at[g]).wait()
        send_blocks(pv.at[g], xp.at[g, 1], s1p_send.at[g], s1p_recv.at[g])
        xp[g, 1, p] = pv[g, p]
    lanes = lax.broadcasted_iota(jnp.int32, (1, modes_total), 1)
    own_mode = jnp.sum(jnp.where(lanes == i, slot_f, 0.0), axis=1, keepdims=True)
    own_rank = jnp.sum(
        jnp.where(lanes.astype(F32) == own_mode, rank_v[...].astype(F32), 0.0), axis=1, keepdims=True
    )
    levels = eigen_v.shape[1]
    eig = column_of(eigen_v[...], levels)
    level = lax.broadcasted_iota(jnp.int32, (levels, 1), 0).astype(F32)
    weight = jnp.where(level < own_rank, eig / (1.0 + eig), 0.0)

    def partial_modes(block, q):
        return jnp.dot(tab[q, 0], block, preferred_element_type=F32) + jnp.dot(
            tab[q, 1], block, preferred_element_type=F32
        )

    def store_parts(s, res):
        m = modes_total
        cr, ci, sr, si = res[:m, :W], res[:m, W:], res[m:, :W], res[m:, W:]
        for n, v in enumerate((cr + si, ci - sr, cr - si, ci + sr)):
            part[s, :, n] = v.astype(BF16).reshape(NZ, NP, W)

    def transform(s):
        blocks = pl.ds(0, NP - 1)
        pltpu.make_async_copy(xs.at[s, blocks], xs.at[s, blocks], s1_recv.at[s]).wait()
        store_parts(s, partial_modes(xs[s].reshape(plane_times, 2 * W), 0))

    def pair_start(g):
        blocks = pl.ds(0, NP - 1)
        pltpu.make_async_copy(xp.at[g, :, blocks], xp.at[g, :, blocks], s1p_recv.at[g]).wait()
        store_parts(
            SINGLES + g,
            partial_modes(xp[g, 0].reshape(plane_times, 2 * W), 0)
            + partial_modes(xp[g, 1].reshape(plane_times, 2 * W), 1 + g),
        )
        for n, d in enumerate(PAIR_HOPS):
            pltpu.make_async_remote_copy(
                src_ref=part.at[SINGLES + g, zrow(d)], dst_ref=zp.at[g, n], send_sem=zp_send.at[g],
                recv_sem=zp_recv.at[g], device_id=zdev(d), device_id_type=MESH,
            ).start()

    def pair_end(g):
        pltpu.make_async_copy(zp.at[g], zp.at[g], zp_recv.at[g]).wait()
        mine = part[SINGLES + g, z].astype(F32)
        others = jnp.zeros_like(mine)
        for n, d in enumerate(PAIR_HOPS):
            if d % 2 == 0:
                mine = mine + zp[g, n].astype(F32)
            else:
                others = others + zp[g, n].astype(F32)
        first = jnp.where(upper[g] == 0, mine, others)
        second = jnp.where(upper[g] == 0, others, mine)
        for m, v in enumerate((first, second)):
            s = SINGLES + 2 * g + m
            for n in range(4):
                fsum[s // GSUB, :, (s % GSUB) * 4 + n, :] = v[n]

    def z_step(s, k):
        last, sends, counts, arrivals = z_plan(s)
        if k == 0:
            transform(s)
        else:
            some = pl.ds(0, counts[k])
            pltpu.make_async_copy(zbuf.at[s, some], zbuf.at[s, some], z_recv.at[s, k]).wait()
        if k == last:
            v = part[s, z].astype(F32)
            for slot in arrivals:
                v = v + zbuf[s, slot].astype(F32)
            for n in range(4):
                fsum[s // GSUB, :, (s % GSUB) * 4 + n, :] = v[n]
            return
        for slot, sign, d, to, to_level, below in sends[k]:
            src = part.at[s, zrow(sign * d)]
            if below:
                v = src[...].astype(F32)
                for c in below:
                    v = v + zbuf[s, c].astype(F32)
                src = bbuf.at[s, slot]
                src[...] = v.astype(BF16)
            pltpu.make_async_remote_copy(
                src_ref=src, dst_ref=zbuf.at[s, slot], send_sem=z_send.at[s], recv_sem=z_recv.at[s, to_level],
                device_id=zdev(sign * (d - to)), device_id_type=MESH,
            ).start()

    def exchange(g):
        ob[g] = fsum[g].astype(BF16)
        for n, (dx, dy) in enumerate(offsets):
            to = plane(dx, dy)
            pltpu.make_async_remote_copy(
                src_ref=ob.at[g, to], dst_ref=modes.at[g, p], send_sem=s3_send.at[g],
                recv_sem=s3_recv.at[g, n], device_id={"ma": z * NP + to}, device_id_type=MESH,
            ).start()

    baselines = vis.shape[2]

    def project_one(b, rows, g, acc):
        for s in range(GSUB):
            for n in range(4):
                at = pl.multiple_of(n * baselines + b * (NSUB * W) + (g * GSUB + s) * W, W)
                r = s * 4 + n
                acc = acc + beam_v[:, pl.ds(at, W)].astype(F32) * rows[r:r + 1, :]
        return acc

    def project(g, acc):
        acc = project_one(p, ob[g, p].astype(F32), g, acc)
        for n in reversed(range(len(offsets))):
            dx, dy = offsets[n]
            b = plane(NX - dx, NY - dy)
            pltpu.make_async_copy(modes.at[g, b], modes.at[g, b], s3_recv.at[g, n]).wait()
            acc = project_one(b, modes[g, b].astype(F32), g, acc)
        return acc

    done = [0] * NG
    for s, k in schedule():
        finished = []
        if k == "start":
            pair_start(s)
        elif k == "end":
            pair_end(s)
            finished = [SINGLES + 2 * s, SINGLES + 2 * s + 1]
        else:
            z_step(s, k)
            finished = [s] if k == z_plan(s)[0] else []
        for f in finished:
            g = f // GSUB
            done[g] += 1
            if done[g] == GSUB:
                exchange(g)
    pltpu.make_async_copy(beam.at[0], beam_v, beam_sem).wait()
    pltpu.make_async_copy(sky.at[0], sky_v, sky_sem).wait()
    acc = jnp.zeros((levels, W), F32)
    for g in range(NG):
        acc = project(g, acc)
    filtered = jnp.sum(acc, axis=1, keepdims=True) * weight
    out[...] = jnp.sum(sky_v[...].astype(F32) * filtered, axis=0, keepdims=True)

    for s in range(SINGLES):
        blocks = pl.ds(0, NP - 1)
        pltpu.make_async_copy(vb.at[s, blocks], vb.at[s, blocks], s1_send.at[s]).wait()
        pltpu.make_async_copy(zbuf.at[s], zbuf.at[s], z_send.at[s]).wait()
    for g in range(PAIRS):
        blocks = pl.ds(0, NP - 1)
        pltpu.make_async_copy(pv.at[g], pv.at[g], pair_send.at[g]).wait()
        pltpu.make_async_copy(xp.at[g, :, blocks], xp.at[g, :, blocks], s1p_send.at[g]).wait()
        pltpu.make_async_copy(zp.at[g], zp.at[g], zp_send.at[g]).wait()
    for g in range(NG):
        blocks = pl.ds(0, NP - 1)
        pltpu.make_async_copy(ob.at[g, blocks], ob.at[g, blocks], s3_send.at[g]).wait()


def per_device(visibility, slot_mode, mode_rank, beam_svd, signal_eigen, sky_map):
    count = slot_mode.shape[0]
    levels, entries = beam_svd.shape[1:]
    multipoles = sky_map.shape[2]
    times = visibility.shape[1]
    any_spec = pl.BlockSpec(memory_space=pl.ANY)
    dma = pltpu.SemaphoreType.DMA
    return pl.pallas_call(
        kernel,
        out_shape=jax.ShapeDtypeStruct((1, multipoles), F32),
        in_specs=[any_spec] * 6,
        out_specs=pl.BlockSpec(memory_space=pltpu.VMEM),
        scratch_shapes=[
            pltpu.VMEM(visibility.shape, F32),
            pltpu.VMEM((1, count), jnp.int32),
            pltpu.VMEM((1, count), jnp.int32),
            pltpu.VMEM((levels, entries), BF16),
            pltpu.VMEM((1, levels), F32),
            pltpu.VMEM((levels, multipoles), BF16),
            pltpu.VMEM((NSUB, NP, times, 2 * W), BF16),
            pltpu.VMEM((NSUB, NP, times, 2 * W), BF16),
            pltpu.VMEM((1 + PAIRS, 2, 2 * count, times * NP), BF16),
            pltpu.VMEM((NSUB, NZ, 4, NP, W), BF16),
            pltpu.VMEM((NSUB, 7, 4, NP, W), BF16),
            pltpu.VMEM((NSUB, 7, 4, NP, W), BF16),
            pltpu.VMEM((NG, NP, 4 * GSUB, W), F32),
            pltpu.VMEM((NG, NP, 4 * GSUB, W), BF16),
            pltpu.VMEM((NG, NP, 4 * GSUB, W), BF16),
            dma((4,)), dma((3,)), dma, dma,
            dma((NSUB,)), dma((NSUB,)), dma((NSUB,)), dma((NSUB, LEVELS)), dma((NG,)), dma((NG, NP - 1)),
            pltpu.VMEM((PAIRS, NP, times, 2 * W), BF16),
            pltpu.VMEM((PAIRS, 2, NP, times, 2 * W), BF16),
            pltpu.VMEM((PAIRS, NZ - 1, 4, NP, W), BF16),
            dma((PAIRS,)), dma((PAIRS,)), dma((PAIRS,)), dma((PAIRS,)), dma((PAIRS,)), dma((PAIRS,)),
        ],
        compiler_params=pltpu.CompilerParams(
            collective_id=0, has_side_effects=True, vmem_limit_bytes=60 * 2**20
        ),
    )(
        visibility, slot_mode.reshape(1, count), mode_rank.reshape(1, count), beam_svd, signal_eigen, sky_map
    )


def solution(mesh):
    return jax.shard_map(
        per_device,
        mesh=mesh,
        in_specs=(
            P("freq", "ma", None),
            P(),
            P(),
            P(("freq", "ma"), None, None),
            P(("freq", "ma"), None),
            P(("freq", "ma"), None, None),
        ),
        out_specs=P(("freq", "ma"), None),
        check_vma=False,
    )
```

```python
import functools
import math

import jax
import jax.numpy as jnp
from jax import lax
from jax.experimental import pallas as pl
from jax.experimental.pallas import tpu as pltpu
from jax.sharding import PartitionSpec as P

MESH = pl.DeviceIdType.MESH
NZ, NX, NY = 8, 4, 4
NP = NX * NY
NSUB = 8
GSUB = 4
NG = NSUB // GSUB
W = 128
F32, BF16 = jnp.float32, jnp.bfloat16

CHAIN = {4: 3, 3: 2, 2: 1, 1: 0}
THREE = {4: 3, 3: 1, 2: 1, 1: 0}
TREE = {4: 2, 3: 2, 2: 0, 1: 0}
DIRECT = {4: 0, 3: 0, 2: 0, 1: 0}
SINGLES = 4
PAIRS = (NSUB - SINGLES) // 2
PLANS = (TREE,) * SINGLES
LEVELS = 5
PAIR_HOPS = (4, 3, -3, 2, -2, 1, -1)
NODES = ((1, 3), (-1, 3), (0, 4), (1, 2), (-1, 2), (1, 1), (-1, 1))


def z_plan(s):
    sign4 = 1 if s % 2 == 0 else -1
    parent = PLANS[s]
    nodes = [(side or sign4, d, slot) for slot, (side, d) in enumerate(NODES)]

    def children(sign, d):
        return [n for n in nodes if d and n[0] == sign and parent[n[1]] == d]

    def level(sign, d):
        below = [n for n in nodes if parent[n[1]] == 0] if d == 0 else children(sign, d)
        return max((1 + level(n[0], n[1]) for n in below), default=0)

    last = level(0, 0)
    sends = [[] for _ in range(last)]
    counts = [0] * (last + 1)
    for sign, d, slot in nodes:
        to = parent[d]
        to_level = level(sign if to else 0, to)
        counts[to_level] += 1
        sends[level(sign, d)].append((slot, sign, d, to, to_level, [n[2] for n in children(sign, d)]))
    for group in sends:
        group.sort(key=lambda n: -n[2])
    arrivals = [n[2] for n in nodes if parent[n[1]] == 0]
    return last, sends, counts, arrivals


def schedule():
    events = []
    for s in range(SINGLES):
        for k in range(z_plan(s)[0] + 1):
            events.append((S_EACH * s + (FIRST + LATER * (k - 1) if k else 0.0), s, k))
    for g in range(PAIRS):
        t = S_EACH * (SINGLES + 1 + 2 * g)
        events += [(t, g, "start"), (t + PAIR_COPY, g, "end")]
    return [(s, k) for _, s, k in sorted(events, key=lambda e: e[0])]


S_EACH, FIRST, LATER, PAIR_COPY = 1.43, 4.2, 4.6, 8.0


def sin_cos(index, period):
    quarter = period // 4
    shifted = index + quarter // 2
    quadrant = (shifted // quarter) % 4
    small = (shifted % quarter) - quarter // 2
    a = small.astype(F32) * F32(2.0 * math.pi / period)
    a2 = a * a
    s = a * (1.0 + a2 * (-1.0 / 6 + a2 * (1.0 / 120 + a2 * (-1.0 / 5040 + a2 * (1.0 / 362880)))))
    c = 1.0 + a2 * (-0.5 + a2 * (1.0 / 24 + a2 * (-1.0 / 720 + a2 * (1.0 / 40320))))
    odd = (quadrant % 2) == 1
    sin = jnp.where(odd, c, s)
    cos = jnp.where(odd, s, c)
    sin = jnp.where(quadrant >= 2, -sin, sin)
    cos = jnp.where((quadrant == 1) | (quadrant == 2), -cos, cos)
    return sin, cos


def column_of(row, n):
    r = lax.broadcasted_iota(jnp.int32, (n, n), 0)
    c = lax.broadcasted_iota(jnp.int32, (n, n), 1)
    return jnp.sum(jnp.where(r == c, jnp.broadcast_to(row, (n, n)), 0.0), axis=1, keepdims=True)


def kernel(
    vis, slot, rank, beam, eigen, sky, out,
    vis_v, slot_v, rank_v, beam_v, eigen_v, sky_v,
    vb, xs, tab, part, zbuf, bbuf, fsum, ob, modes,
    vis_sem, small_sem, beam_sem, sky_sem,
    s1_send, s1_recv, z_send, z_recv, s3_send, s3_recv,
    pv, xp, zp, pair_send, pair_recv, s1p_send, s1p_recv, zp_send, zp_recv,
):
    i = lax.axis_index("ma")
    z, p = i // NP, i % NP
    x, y = p // NY, p % NY
    modes_total = slot.shape[1]
    times = vis.shape[1]
    total = times * NZ * NP
    plane_times = times * NP

    def plane(dx, dy):
        return ((x + dx) % NX) * NY + (y + dy) % NY

    def zdev(d):
        return {"ma": ((z + d + NZ) % NZ) * NP + p}

    offsets = sorted(
        ((dx, dy) for dx in range(NX) for dy in range(NY) if (dx, dy) != (0, 0)),
        key=lambda o: -min(o[0], NX - o[0]) - min(o[1], NY - o[1]),
    )
    hops = {sign * (d - to) for s in range(SINGLES) for group in z_plan(s)[1] for _, sign, d, to, _, _ in group}
    hops |= set(range(1, NZ)) if PAIRS else set()
    zoffs = sorted({h % NZ for h in hops} | {-h % NZ for h in hops})

    pieces = vis_sem.shape[0]
    span = vis.shape[2] // pieces
    for q in range(pieces):
        cols = pl.ds(q * span, span)
        pltpu.make_async_copy(vis.at[:, :, cols], vis_v.at[:, :, cols], vis_sem.at[q]).start()
    small = [(slot, slot_v), (rank, rank_v), (eigen, eigen_v)]
    for n, (src, dst) in enumerate(small):
        pltpu.make_async_copy(src, dst, small_sem.at[n]).start()

    def zrow(d):
        return (z + d + NZ) % NZ

    barrier = pltpu.get_barrier_semaphore()
    for dx, dy in offsets:
        pl.semaphore_signal(barrier, 1, device_id={"ma": z * NP + plane(dx, dy)}, device_id_type=MESH)
    for d in zoffs:
        pl.semaphore_signal(barrier, 1, device_id=zdev(d), device_id_type=MESH)

    for q in range(pieces):
        cols = pl.ds(q * span, span)
        pltpu.make_async_copy(vis.at[:, :, cols], vis_v.at[:, :, cols], vis_sem.at[q]).wait()

        def cast(b, carry):
            for s in range(NSUB):
                for c in range(2):
                    at = pl.multiple_of(b * (NSUB * W) + s * W, W)
                    vb[s, b, :, c * W:(c + 1) * W] = vis_v[c, :, pl.ds(at, W)].astype(BF16)
            return carry

        per = NP // pieces
        lax.fori_loop(q * per, (q + 1) * per, cast, 0)
    pltpu.make_async_copy(beam.at[0], beam_v, beam_sem).start()
    pltpu.make_async_copy(sky.at[0], sky_v, sky_sem).start()

    pl.semaphore_wait(barrier, len(offsets) + len(zoffs))
    upper = [(z + g) % 2 for g in range(PAIRS)]
    kept = [SINGLES + 2 * g + upper[g] for g in range(PAIRS)]
    given = [SINGLES + 2 * g + 1 - upper[g] for g in range(PAIRS)]
    other = [1 - 2 * upper[g] for g in range(PAIRS)]

    for g in range(PAIRS):
        pltpu.make_async_remote_copy(
            src_ref=vb.at[given[g]], dst_ref=pv.at[g], send_sem=pair_send.at[g], recv_sem=pair_recv.at[g],
            device_id=zdev(other[g]), device_id_type=MESH,
        ).start()

    def send_blocks(src, dst, send_sem, recv_sem):
        for dx, dy in offsets:
            to = plane(dx, dy)
            pltpu.make_async_remote_copy(
                src_ref=src.at[to], dst_ref=dst.at[p], send_sem=send_sem, recv_sem=recv_sem,
                device_id={"ma": z * NP + to}, device_id_type=MESH,
            ).start()

    def send_single(s, carry):
        send_blocks(vb.at[s], xs.at[s], s1_send.at[s], s1_recv.at[s])
        return carry

    for s in range(SINGLES):
        send_single(s, 0)
    send_blocks(vb.at[kept[0]], xp.at[0, 0], s1p_send.at[0], s1p_recv.at[0])

    for s in range(SINGLES):
        xs[s, p] = vb[s, p]
    for g in range(PAIRS):
        xp[g, 0, p] = vb[kept[g], p]
    for n, (src, dst) in enumerate(small):
        pltpu.make_async_copy(src, dst, small_sem.at[n]).wait()
    slot_f = slot_v[...].astype(F32)
    wave = (column_of(slot_f, modes_total) + 1.0).astype(jnp.int32)
    scale = F32(1.0 / math.sqrt(total))
    for q, d in enumerate([0] + other):
        t = zrow(d) * plane_times + lax.broadcasted_iota(jnp.int32, (modes_total, plane_times), 1)
        sin, cos = sin_cos((wave * t) % total, total)
        for n, table in enumerate((cos * scale, sin * scale)):
            high = table.astype(BF16)
            rows = pl.ds(n * modes_total, modes_total)
            tab[q, 0, rows, :] = high
            tab[q, 1, rows, :] = (table - high.astype(F32)).astype(BF16)
    for g in range(PAIRS):
        pltpu.make_async_copy(pv.at[g], pv.at[g], pair_recv.at[g]).wait()
        send_blocks(pv.at[g], xp.at[g, 1], s1p_send.at[g], s1p_recv.at[g])
        if g + 1 < PAIRS:
            send_blocks(vb.at[kept[g + 1]], xp.at[g + 1, 0], s1p_send.at[g + 1], s1p_recv.at[g + 1])
        xp[g, 1, p] = pv[g, p]
    lanes = lax.broadcasted_iota(jnp.int32, (1, modes_total), 1)
    own_mode = jnp.sum(jnp.where(lanes == i, slot_f, 0.0), axis=1, keepdims=True)
    own_rank = jnp.sum(
        jnp.where(lanes.astype(F32) == own_mode, rank_v[...].astype(F32), 0.0), axis=1, keepdims=True
    )
    levels = eigen_v.shape[1]
    eig = column_of(eigen_v[...], levels)
    level = lax.broadcasted_iota(jnp.int32, (levels, 1), 0).astype(F32)
    weight = jnp.where(level < own_rank, eig / (1.0 + eig), 0.0)

    def partial_modes(block, q):
        return jnp.dot(tab[q, 0], block, preferred_element_type=F32) + jnp.dot(
            tab[q, 1], block, preferred_element_type=F32
        )

    def store_parts(s, res):
        m = modes_total
        cr, ci, sr, si = res[:m, :W], res[:m, W:], res[m:, :W], res[m:, W:]
        for n, v in enumerate((cr + si, ci - sr, cr - si, ci + sr)):
            part[s, :, n] = v.astype(BF16).reshape(NZ, NP, W)

    def transform(s):
        blocks = pl.ds(0, NP - 1)
        pltpu.make_async_copy(xs.at[s, blocks], xs.at[s, blocks], s1_recv.at[s]).wait()
        store_parts(s, partial_modes(xs[s].reshape(plane_times, 2 * W), 0))

    def pair_start(g):
        blocks = pl.ds(0, NP - 1)
        pltpu.make_async_copy(xp.at[g, :, blocks], xp.at[g, :, blocks], s1p_recv.at[g]).wait()
        store_parts(
            SINGLES + g,
            partial_modes(xp[g, 0].reshape(plane_times, 2 * W), 0)
            + partial_modes(xp[g, 1].reshape(plane_times, 2 * W), 1 + g),
        )
        for n, d in enumerate(PAIR_HOPS):
            pltpu.make_async_remote_copy(
                src_ref=part.at[SINGLES + g, zrow(d)], dst_ref=zp.at[g, n], send_sem=zp_send.at[g],
                recv_sem=zp_recv.at[g], device_id=zdev(d), device_id_type=MESH,
            ).start()

    def pair_end(g):
        pltpu.make_async_copy(zp.at[g], zp.at[g], zp_recv.at[g]).wait()
        mine = part[SINGLES + g, z].astype(F32)
        others = jnp.zeros_like(mine)
        for n, d in enumerate(PAIR_HOPS):
            if d % 2 == 0:
                mine = mine + zp[g, n].astype(F32)
            else:
                others = others + zp[g, n].astype(F32)
        first = jnp.where(upper[g] == 0, mine, others)
        second = jnp.where(upper[g] == 0, others, mine)
        for m, v in enumerate((first, second)):
            s = SINGLES + 2 * g + m
            for n in range(4):
                fsum[s // GSUB, :, (s % GSUB) * 4 + n, :] = v[n]

    def z_step(s, k):
        last, sends, counts, arrivals = z_plan(s)
        if k == 0:
            transform(s)
        else:
            some = pl.ds(0, counts[k])
            pltpu.make_async_copy(zbuf.at[s, some], zbuf.at[s, some], z_recv.at[s, k]).wait()
        if k == last:
            v = part[s, z].astype(F32)
            for slot in arrivals:
                v = v + zbuf[s, slot].astype(F32)
            for n in range(4):
                fsum[s // GSUB, :, (s % GSUB) * 4 + n, :] = v[n]
            return
        for slot, sign, d, to, to_level, below in sends[k]:
            src = part.at[s, zrow(sign * d)]
            if below:
                v = src[...].astype(F32)
                for c in below:
                    v = v + zbuf[s, c].astype(F32)
                src = bbuf.at[s, slot]
                src[...] = v.astype(BF16)
            pltpu.make_async_remote_copy(
                src_ref=src, dst_ref=zbuf.at[s, slot], send_sem=z_send.at[s], recv_sem=z_recv.at[s, to_level],
                device_id=zdev(sign * (d - to)), device_id_type=MESH,
            ).start()

    def exchange(g):
        ob[g] = fsum[g].astype(BF16)
        for n, (dx, dy) in enumerate(offsets):
            to = plane(dx, dy)
            pltpu.make_async_remote_copy(
                src_ref=ob.at[g, to], dst_ref=modes.at[g, p], send_sem=s3_send.at[g],
                recv_sem=s3_recv.at[g, n], device_id={"ma": z * NP + to}, device_id_type=MESH,
            ).start()

    baselines = vis.shape[2]

    def project_one(b, rows, g, acc):
        for s in range(GSUB):
            for n in range(4):
                at = pl.multiple_of(n * baselines + b * (NSUB * W) + (g * GSUB + s) * W, W)
                r = s * 4 + n
                acc = acc + beam_v[:, pl.ds(at, W)].astype(F32) * rows[r:r + 1, :]
        return acc

    def project(g, acc):
        acc = project_one(p, ob[g, p].astype(F32), g, acc)
        for n in reversed(range(len(offsets))):
            dx, dy = offsets[n]
            b = plane(NX - dx, NY - dy)
            pltpu.make_async_copy(modes.at[g, b], modes.at[g, b], s3_recv.at[g, n]).wait()
            acc = project_one(b, modes[g, b].astype(F32), g, acc)
        return acc

    done = [0] * NG
    for s, k in schedule():
        finished = []
        if k == "start":
            pair_start(s)
        elif k == "end":
            pair_end(s)
            finished = [SINGLES + 2 * s, SINGLES + 2 * s + 1]
        else:
            z_step(s, k)
            finished = [s] if k == z_plan(s)[0] else []
        for f in finished:
            g = f // GSUB
            done[g] += 1
            if done[g] == GSUB:
                exchange(g)
    pltpu.make_async_copy(beam.at[0], beam_v, beam_sem).wait()
    pltpu.make_async_copy(sky.at[0], sky_v, sky_sem).wait()
    acc = jnp.zeros((levels, W), F32)
    for g in range(NG):
        acc = project(g, acc)
    filtered = jnp.sum(acc, axis=1, keepdims=True) * weight
    out[...] = jnp.sum(sky_v[...].astype(F32) * filtered, axis=0, keepdims=True)

    for s in range(SINGLES):
        blocks = pl.ds(0, NP - 1)
        pltpu.make_async_copy(vb.at[s, blocks], vb.at[s, blocks], s1_send.at[s]).wait()
        pltpu.make_async_copy(zbuf.at[s], zbuf.at[s], z_send.at[s]).wait()
    for g in range(PAIRS):
        blocks = pl.ds(0, NP - 1)
        pltpu.make_async_copy(pv.at[g], pv.at[g], pair_send.at[g]).wait()
        pltpu.make_async_copy(xp.at[g, :, blocks], xp.at[g, :, blocks], s1p_send.at[g]).wait()
        pltpu.make_async_copy(zp.at[g], zp.at[g], zp_send.at[g]).wait()
    for g in range(NG):
        blocks = pl.ds(0, NP - 1)
        pltpu.make_async_copy(ob.at[g, blocks], ob.at[g, blocks], s3_send.at[g]).wait()


def per_device(visibility, slot_mode, mode_rank, beam_svd, signal_eigen, sky_map):
    count = slot_mode.shape[0]
    levels, entries = beam_svd.shape[1:]
    multipoles = sky_map.shape[2]
    times = visibility.shape[1]
    any_spec = pl.BlockSpec(memory_space=pl.ANY)
    dma = pltpu.SemaphoreType.DMA
    return pl.pallas_call(
        kernel,
        out_shape=jax.ShapeDtypeStruct((1, multipoles), F32),
        in_specs=[any_spec] * 6,
        out_specs=pl.BlockSpec(memory_space=pltpu.VMEM),
        scratch_shapes=[
            pltpu.VMEM(visibility.shape, F32),
            pltpu.VMEM((1, count), jnp.int32),
            pltpu.VMEM((1, count), jnp.int32),
            pltpu.VMEM((levels, entries), BF16),
            pltpu.VMEM((1, levels), F32),
            pltpu.VMEM((levels, multipoles), BF16),
            pltpu.VMEM((NSUB, NP, times, 2 * W), BF16),
            pltpu.VMEM((NSUB, NP, times, 2 * W), BF16),
            pltpu.VMEM((1 + PAIRS, 2, 2 * count, times * NP), BF16),
            pltpu.VMEM((NSUB, NZ, 4, NP, W), BF16),
            pltpu.VMEM((NSUB, 7, 4, NP, W), BF16),
            pltpu.VMEM((NSUB, 7, 4, NP, W), BF16),
            pltpu.VMEM((NG, NP, 4 * GSUB, W), F32),
            pltpu.VMEM((NG, NP, 4 * GSUB, W), BF16),
            pltpu.VMEM((NG, NP, 4 * GSUB, W), BF16),
            dma((4,)), dma((3,)), dma, dma,
            dma((NSUB,)), dma((NSUB,)), dma((NSUB,)), dma((NSUB, LEVELS)), dma((NG,)), dma((NG, NP - 1)),
            pltpu.VMEM((PAIRS, NP, times, 2 * W), BF16),
            pltpu.VMEM((PAIRS, 2, NP, times, 2 * W), BF16),
            pltpu.VMEM((PAIRS, NZ - 1, 4, NP, W), BF16),
            dma((PAIRS,)), dma((PAIRS,)), dma((PAIRS,)), dma((PAIRS,)), dma((PAIRS,)), dma((PAIRS,)),
        ],
        compiler_params=pltpu.CompilerParams(
            collective_id=0, has_side_effects=True, vmem_limit_bytes=60 * 2**20
        ),
    )(
        visibility, slot_mode.reshape(1, count), mode_rank.reshape(1, count), beam_svd, signal_eigen, sky_map
    )


def solution(mesh):
    return jax.shard_map(
        per_device,
        mesh=mesh,
        in_specs=(
            P("freq", "ma", None),
            P(),
            P(),
            P(("freq", "ma"), None, None),
            P(("freq", "ma"), None),
            P(("freq", "ma"), None, None),
        ),
        out_specs=P(("freq", "ma"), None),
        check_vma=False,
    )
```
